32 devices in a mesh: dp: 2 (over x), row: 2 (over core), col: 8 (over z, y).
Axes of the slice: x: 2, y: 2, z: 4, core: 2. Of those that a mesh axis runs over, the one named last changes fastest.
Arguments:
- features: bfloat16 [2, 48, 192, 256], P('dp', 'row', 'col'), may hold values from -8.5 to 8.5
- cotangent: bfloat16 [2, 48, 192, 256], P('dp', 'row', 'col'), may hold values from -4.5 to 4.5
- w_one: bfloat16 [256, 256], replicated, may hold values from -0.375 to 0.375
- w_point: bfloat16 [3, 256, 256], replicated, may hold values from -0.375 to 0.375
- taps: float32 [3, 3, 3, 256], replicated, may hold values from -2 to 2
- w_pool: bfloat16 [256, 256], replicated, may hold values from -0.375 to 0.375
- w_proj: bfloat16 [1280, 256], replicated, may hold values from -0.15625 to 0.15625
Outputs:
- mixed: bfloat16 [2, 48, 192, 256], P('dp', 'row', 'col')
- grad_input: bfloat16 [2, 48, 192, 256], P('dp', 'row', 'col')
- grad_one: float32 [256, 256], replicated
- grad_point: float32 [3, 256, 256], replicated
- grad_taps: float32 [3, 3, 3, 256], replicated
- grad_pool: float32 [256, 256], replicated
- grad_proj: float32 [1280, 256], replicated
The draws below stay inside these ranges and needn't reach their ends.
All inputs are finite; a program needn't handle non-finite values.
Results may differ from the reference program's by a relative error of at most 0.0079.
Values may be sent and summed in bfloat16 or wider, within the bound.
A program may use at most 64 MiB of HBM per device.

```python
import math
import jax
import jax.numpy as jnp
from jax import lax

C_IN = 256
C = 256
CAT = 1280
IMAGES = 2
NR = 48
NC = 192


def position_ramp():
    rows = jnp.arange(NR, dtype=jnp.float32) / max(NR - 1, 1)
    cols = jnp.arange(NC, dtype=jnp.float32) / max(NC - 1, 1)
    return (rows[:, None] + cols[None, :])[None, :, :, None]


def draw_features(key, part):
    key = jax.random.fold_in(key, 11)
    key_mean, key_noise = jax.random.split(key, 2)
    ramp = 1.0 + position_ramp()
    means = jax.random.uniform(key_mean, (C_IN,), jnp.float32, -1.5, 1.5)
    noise = jax.random.truncated_normal(key_noise, -4.0, 4.0, (IMAGES, NR, NC, C_IN), jnp.float32)
    values = means * ramp + noise
    return values.astype(jnp.bfloat16)


def draw_cotangent(key, part):
    key = jax.random.fold_in(key, 23)
    ramp = 0.5 + 0.5 * position_ramp()
    noise = jax.random.truncated_normal(key, -3.0, 3.0, (IMAGES, NR, NC, C), jnp.float32)
    return (noise * ramp).astype(jnp.bfloat16)


def normal_values(own_key, dims, spread, reach, kind=jnp.bfloat16):
    drawn = jax.random.normal(own_key, dims, jnp.float32) * spread
    return jnp.minimum(jnp.maximum(drawn, -reach), reach).astype(kind)


def setup_inputs(seed: int = 0) -> dict:
    streams_of = jax.random.split(jax.random.key(seed), 8)
    features = draw_features(jax.random.fold_in(streams_of[7], 71), 0)
    cotangent = draw_cotangent(jax.random.fold_in(streams_of[7], 71), 0)
    w_one = normal_values(streams_of[2], (C_IN, C), C_IN ** -0.5, 0.375)
    w_point = normal_values(streams_of[3], (3, C_IN, C), C_IN ** -0.5, 0.375)
    taps = normal_values(streams_of[4], (3, 3, 3, C_IN), 9 ** -0.5, 2.0, jnp.float32)
    w_pool = normal_values(streams_of[5], (C_IN, C), C_IN ** -0.5, 0.375)
    w_proj = normal_values(streams_of[6], (CAT, C), CAT ** -0.5, 0.15625)
    return dict(features=features, cotangent=cotangent, w_one=w_one, w_point=w_point, taps=taps, w_pool=w_pool, w_proj=w_proj)


dilations = (6, 12, 18)
margin = 18

def silu_parts(value):
    sig = jax.nn.sigmoid(value)
    return (value * sig, sig * (1.0 + value * (1.0 - sig)))

def depthwise(padded, weights, rate, rows, cols, offset_sign):
    total = jnp.zeros((rows, cols, padded.shape[-1]), jnp.float32)
    for i in range(3):
        for j in range(3):
            top = margin + offset_sign * rate * (i - 1)
            left = margin + offset_sign * rate * (j - 1)
            window = padded[top:top + rows, left:left + cols, :].astype(jnp.float32)
            total = total + window * weights[i, j]
    return total

def reference(features, cotangent, w_one, w_point, taps, w_pool, w_proj):
    highest = lax.Precision.HIGHEST
    npos = NR * NC
    main = w_proj[:4 * C]
    last = w_proj[4 * C:].astype(jnp.float32)
    pool32 = w_pool.astype(jnp.float32)

    def one_image(carry, pair):
        image, cot = pair
        padded = jnp.pad(image, ((margin, margin), (margin, margin), (0, 0)))
        flat = image.reshape(npos, C_IN)
        u_zero = jnp.dot(flat, w_one, preferred_element_type=jnp.float32)
        act, slope = silu_parts(u_zero)
        acts = [act.astype(jnp.bfloat16)]
        slopes = [slope]
        inner = []
        for k in range(3):
            depth_out = depthwise(padded, taps[k], dilations[k], NR, NC, 1).astype(jnp.bfloat16).reshape(npos, C_IN)
            u_k = jnp.dot(depth_out, w_point[k], preferred_element_type=jnp.float32)
            act, slope = silu_parts(u_k)
            acts.append(act.astype(jnp.bfloat16))
            slopes.append(slope)
            inner.append(depth_out)
        pooled = (lax.optimization_barrier(jnp.sum(image.astype(jnp.float32), axis=(0, 1))) / npos).reshape(1, C_IN)
        q_val = jnp.dot(pooled, pool32, precision=highest)
        a_four, s_four = silu_parts(q_val)
        joined = jnp.concatenate(acts, axis=1)
        pre = jnp.dot(joined, main, preferred_element_type=jnp.float32) + jnp.dot(a_four, last, precision=highest)
        mixed, s_pre = silu_parts(pre)
        dpre = (cot.reshape(npos, C).astype(jnp.float32) * s_pre).astype(jnp.bfloat16)
        slope_total = lax.optimization_barrier(jnp.sum(dpre.astype(jnp.float32), axis=0)).reshape(1, C)
        grad_main = jnp.dot(joined.T, dpre, preferred_element_type=jnp.float32)
        dcat = jnp.dot(dpre, main.T, preferred_element_type=jnp.float32)
        dus = [(dcat[:, m * C:(m + 1) * C] * slopes[m]).astype(jnp.bfloat16) for m in range(4)]
        g_one = jnp.dot(flat.T, dus[0], preferred_element_type=jnp.float32)
        g_point = jnp.stack([jnp.dot(inner[k].T, dus[k + 1], preferred_element_type=jnp.float32) for k in range(3)])
        dq = jnp.dot(slope_total, last.T, precision=highest) * s_four
        dpooled = jnp.dot(dq, pool32.T, precision=highest)
        g_pool = jnp.dot(pooled.T, dq, precision=highest)
        g_four = jnp.dot(a_four.T, slope_total, precision=highest)
        dx = jnp.dot(dus[0], w_one.T, preferred_element_type=jnp.float32).reshape(NR, NC, C_IN)
        tap_list = []
        for k in range(3):
            rate = dilations[k]
            dz = jnp.dot(dus[k + 1], w_point[k].T, preferred_element_type=jnp.float32).astype(jnp.bfloat16).reshape(NR, NC, C_IN)
            dz_pad = jnp.pad(dz, ((margin, margin), (margin, margin), (0, 0)))
            dx = dx + depthwise(dz_pad, taps[k], rate, NR, NC, -1)
            rows_g = []
            for i in range(3):
                cols_g = []
                for j in range(3):
                    top = margin + rate * (i - 1)
                    left = margin + rate * (j - 1)
                    window = padded[top:top + NR, left:left + NC, :].astype(jnp.float32)
                    cols_g.append(jnp.einsum('hwc,hwc->c', window, dz.astype(jnp.float32)))
                rows_g.append(jnp.stack(cols_g))
            tap_list.append(jnp.stack(rows_g))
        dx = dx + (dpooled / npos).reshape(1, 1, C_IN)
        g_proj = jnp.concatenate([grad_main, g_four], axis=0)
        new_carry = (carry[0] + g_one, carry[1] + g_point, carry[2] + jnp.stack(tap_list), carry[3] + g_pool, carry[4] + g_proj)
        outputs = (mixed.astype(jnp.bfloat16).reshape(NR, NC, C), dx.astype(jnp.bfloat16))
        return (new_carry, outputs)
    start = (jnp.zeros((C_IN, C), jnp.float32), jnp.zeros((3, C_IN, C), jnp.float32), jnp.zeros((3, 3, 3, C_IN), jnp.float32), jnp.zeros((C_IN, C), jnp.float32), jnp.zeros((CAT, C), jnp.float32))
    sums, outs = lax.scan(one_image, start, (features, cotangent))
    scale = 1.0 / math.sqrt(IMAGES * NR * NC)
    return (outs[0], outs[1], sums[0] * scale, sums[1] * scale, sums[2] * scale, sums[3] * scale, sums[4] * scale)
```

```python
import functools
import math

import jax
import jax.numpy as jnp
from jax import lax
from jax.experimental import pallas as pl
from jax.experimental.pallas import tpu as pltpu
from jax.sharding import PartitionSpec as P

unit = 6
margin = 18
reach = margin // unit
edge = 112
MESH = pl.DeviceIdType.MESH
f32 = jnp.float32
bf16 = jnp.bfloat16
highest = lax.Precision.HIGHEST


def silu_parts(value):
    sig = jax.nn.sigmoid(value)
    return value * sig, sig * (1.0 + value * (1.0 - sig))


def dot(a, b):
    return jnp.dot(a, b, preferred_element_type=f32)


def dot_nt(a, b):
    return lax.dot_general(a, b, (((1,), (1,)), ((), ())), preferred_element_type=f32)


def dot_tn(a, b):
    return lax.dot_general(a, b, (((0,), (0,)), ((), ())), preferred_element_type=f32)


def fold8(value):
    return jnp.sum(value.reshape(value.shape[0] // 8, 8, value.shape[1]), axis=0)


def kernel(
    n_dp, n_row, n_col, image_cells,
    x_in, cot, w_one, w_point, taps, w_pool, w_proj,
    mixed_out, dx_out, grads_out, taps_out, pool_out, four_out,
    xp, x32, part, slopes, acts, inner, pre_s, dpre_s, du_s, dz_s, dx0,
    slots, images, term, tapacc,
    g32, gb, g_ra, b1, g_rb, b2, g_rc, final,
    t_row, t_dp, t_col,
    row_send, row_recv, col_send, col_recv,
    sm_s, sm_r, xc_s, xc_r, xr_s, xr_r, pr_s, pr_r, pc_s, pc_r,
    ga_s, ga_r, gbs, gbr, gc_s, gc_r, ha_s, ha_r, hb_s, hb_r, hc_s, hc_r,
    ta_s, ta_r, tb_s, tb_r, tc_s, tc_r,
):
    d, r, c = lax.axis_index("dp"), lax.axis_index("row"), lax.axis_index("col")
    total = n_dp * n_row * n_col
    per = n_row * n_col
    me = (d * n_row + r) * n_col + c
    blocks, depth, ch = x_in.shape
    wide = blocks + 2 * reach
    lo, hi = edge, edge + depth

    def peer(i):
        p = lax.rem(me + i, total)
        return {
            "dp": lax.div(p, per),
            "row": lax.rem(lax.div(p, n_col), n_row),
            "col": lax.rem(p, n_col),
        }

    def remote(src, dst, ss, rs, dev):
        return pltpu.make_async_remote_copy(
            src_ref=src, dst_ref=dst, send_sem=ss, recv_sem=rs, device_id=dev, device_id_type=MESH
        )

    barrier = pltpu.get_barrier_semaphore()

    xp[...] = jnp.zeros_like(xp)
    ones = jnp.zeros((8, ch), f32)
    for a in range(blocks):
        block = x_in[a]
        xp[reach + a, lo:hi] = block
        ones = ones + fold8(block.astype(f32))
    slots[0, me] = ones

    @pl.loop(1, total)
    def _(i):
        pl.semaphore_signal(barrier, inc=1, device_id=peer(i), device_id_type=MESH)

    pl.semaphore_wait(barrier, total - 1)

    right, left = {"col": lax.rem(c + 1, n_col)}, {"col": lax.rem(c + n_col - 1, n_col)}
    below, above = {"row": lax.rem(r + 1, n_row)}, {"row": lax.rem(r + n_row - 1, n_row)}
    has_right, has_left = c < n_col - 1, c > 0
    has_below, has_above = r < n_row - 1, r > 0

    def col_copy(side):
        src, dst = (wide - 2 * reach, 0) if side == 0 else (reach, wide - reach)
        mid = pl.ds(lo, depth)
        return remote(
            xp.at[pl.ds(src, reach), mid], xp.at[pl.ds(dst, reach), mid],
            xc_s.at[side], xc_r.at[side], right if side == 0 else left,
        )

    def row_copy(side, seg):
        span = (pl.ds(reach, blocks), pl.ds(0, reach), pl.ds(wide - reach, reach))[seg]
        src, dst = (hi - edge, 0) if side == 0 else (lo, hi)
        return remote(
            xp.at[span, pl.ds(src, edge)], xp.at[span, pl.ds(dst, edge)],
            xr_s.at[side * 3 + seg], xr_r.at[side * 3 + seg], below if side == 0 else above,
        )

    sends = ((has_right, has_left), (has_left, has_right))
    row_sends = ((has_below, has_above), (has_above, has_below))
    for side in range(2):
        @pl.when(sends[side][0])
        def _():
            col_copy(side).start()
    for side in range(2):
        @pl.when(row_sends[side][0])
        def _():
            row_copy(side, 0).start()

    def small_start(which):
        @pl.loop(1, total)
        def _(i):
            remote(
                slots.at[which, me], slots.at[which, me], sm_s.at[which], sm_r.at[which], peer(i)
            ).start()

    def small_wait(which):
        rest = slots.at[which, pl.ds(0, total - 1)]
        remote(rest, rest, sm_s.at[which], sm_r.at[which], peer(1)).wait()

    def small_sums(which):
        images[which] = jnp.zeros((8, ch), f32)
        for b in range(n_dp):
            acc = jnp.sum(slots[which, b * per : (b + 1) * per], axis=0)
            images[which, b : b + 1] = jnp.sum(acc, axis=0, keepdims=True)
        return images[which]

    small_start(0)

    @pl.loop(0, blocks)
    def _(a):
        here = pl.ds(a * depth, depth)
        u = dot(x_in[a], w_one[...])
        act, slope = silu_parts(u)
        act = act.astype(bf16)
        acts[0, here] = act
        slopes[0, here] = slope
        pre_s[here] = dot(act, w_proj[0:ch])

    @pl.loop(0, wide)
    def _(a):
        part[a] = jnp.zeros(part.shape[1:], f32)

    tapacc[...] = jnp.zeros_like(tapacc)

    for side in range(2):
        @pl.when(sends[side][1])
        def _():
            col_copy(side).wait_recv()
            for rside in range(2):
                @pl.when(row_sends[rside][0])
                def _():
                    row_copy(rside, 1 + side).start()

    for side in range(2):
        @pl.when(row_sends[side][1])
        def _():
            row_copy(side, 0).wait_recv()
            for cside in range(2):
                @pl.when(sends[cside][1])
                def _():
                    row_copy(side, 1 + cside).wait_recv()

    @pl.loop(0, wide)
    def _(a):
        x32[a] = xp[a].astype(f32)

    @pl.loop(0, blocks)
    def _(a):
        here = pl.ds(a * depth, depth)
        pre = pre_s[here]
        for k in range(3):
            acc = None
            for i in range(3):
                for j in range(3):
                    row = lo + 36 * (k + 1) * (i - 1)
                    win = x32[a + reach + (k + 1) * (j - 1), row : row + depth]
                    piece = win * taps[k, i, j : j + 1, :]
                    acc = piece if acc is None else acc + piece
            z = acc.astype(bf16)
            inner[k, here] = z
            act, slope = silu_parts(dot(z, w_point[k]))
            act = act.astype(bf16)
            acts[k + 1, here] = act
            slopes[k + 1, here] = slope
            pre = pre + dot(act, w_proj[(k + 1) * ch : (k + 2) * ch])
        pre_s[here] = pre

    small_wait(0)
    pooled = small_sums(0) * (1.0 / image_cells)
    pool32 = w_pool[...].astype(f32)
    last = w_proj[4 * ch : 5 * ch].astype(f32)
    q = jnp.dot(pooled, pool32, precision=highest, preferred_element_type=f32)
    a_four, s_four = silu_parts(q)
    term[...] = jnp.dot(a_four, last, precision=highest, preferred_element_type=f32)
    own_term = term[pl.ds(d, 1), :]

    slots[1, me] = jnp.zeros((8, ch), f32)

    @pl.loop(0, blocks)
    def _(a):
        here = pl.ds(a * depth, depth)
        out, slope = silu_parts(pre_s[here] + own_term)
        mixed_out[a] = out.astype(bf16)
        dpre = (cot[a].astype(f32) * slope).astype(bf16)
        dpre_s[here] = dpre
        slots[1, me] += fold8(dpre.astype(f32))

    small_start(1)

    @pl.loop(0, blocks)
    def _(a):
        here = pl.ds(a * depth, depth)
        dpre = dpre_s[here]
        for m in range(4):
            dcat = dot_nt(dpre, w_proj[m * ch : (m + 1) * ch])
            du = (dcat * slopes[m, here]).astype(bf16)
            du_s[m, here] = du
            if m == 0:
                dx0[a] = dot_nt(du, w_one[...])
            else:
                dz_s[m - 1, here] = dot_nt(du, w_point[m - 1]).astype(bf16)

    for m in range(4):
        g = dot_tn(acts[m], dpre_s[...])
        g32[m * ch : (m + 1) * ch] = g
        gb[m * ch : (m + 1) * ch] = g.astype(bf16)
    for m in range(4):
        g = dot_tn(x_flat(x_in) if m == 0 else inner[m - 1], du_s[m])
        g32[(4 + m) * ch : (5 + m) * ch] = g
        gb[(4 + m) * ch : (5 + m) * ch] = g.astype(bf16)

    whole = g32.shape[0]
    per_row, per_dp, per_col = (
        whole // n_row,
        whole // (n_row * n_dp),
        whole // (n_row * n_dp * n_col),
    )

    def scatter(n, axis, at, size, src, dst, ss, rs):
        out = []
        for i in range(1, n):
            to = lax.rem(at + i, n)
            out.append(
                remote(
                    src.at[pl.ds(pl.multiple_of(to * size, 16), size)], dst.at[i - 1],
                    ss.at[i - 1], rs.at[i - 1], {axis: to},
                )
            )
        return out

    def gather(n, axis, at, base, size, ss, rs):
        own = final.at[pl.ds(pl.multiple_of(base + at * size, 16), size)]
        return [
            remote(own, own, ss.at[i - 1], rs.at[i - 1], {axis: lax.rem(at + i, n)})
            for i in range(1, n)
        ]

    def spread(n, axis, at, buf, ss, rs):
        return [
            remote(buf.at[at], buf.at[at], ss.at[i - 1], rs.at[i - 1], {axis: lax.rem(at + i, n)})
            for i in range(1, n)
        ]

    def start(copies):
        for copy in copies:
            copy.start()

    def wait(copies):
        for copy in copies:
            copy.wait()

    ga = scatter(n_row, "row", r, per_row, gb, g_ra, ga_s, ga_r)
    start(ga)

    @pl.loop(0, blocks)
    def _(a):
        here = pl.ds(a * depth, depth)
        for k in range(3):
            dz = dz_s[k, here].astype(f32)
            for i in range(3):
                for j in range(3):
                    row = lo + 36 * (k + 1) * (i - 1)
                    at = a + reach + (k + 1) * (j - 1)
                    tapacc[9 * k + 3 * i + j] += fold8(x32[at, row : row + depth] * dz)
                    part[at, row : row + depth] += dz * taps[k, i, j : j + 1, :]

    for side in range(2):
        @pl.when(row_sends[side][0])
        def _():
            src = hi if side == 0 else 0
            @pl.loop(0, wide)
            def _(a):
                row_send[side, a] = part[a, src : src + edge].astype(bf16)
            remote(
                row_send.at[side], row_recv.at[side], pr_s.at[side], pr_r.at[side],
                below if side == 0 else above,
            ).start()

    wait(ga)
    mine = pl.multiple_of(r * per_row, 16)
    for s in range(0, per_row, 128):
        acc = g32[pl.ds(pl.multiple_of(mine + s, 16), 128)]
        for i in range(n_row - 1):
            acc = acc + g_ra[i, s : s + 128].astype(f32)
        g32[pl.ds(pl.multiple_of(mine + s, 16), 128)] = acc
        b1[s : s + 128] = acc.astype(bf16)
    gbc = scatter(n_dp, "dp", d, per_dp, b1, g_rb, gbs, gbr)
    start(gbc)

    t_row[r] = jnp.zeros(t_row.shape[1:], f32)
    for t in range(27):
        t_row[r, t : t + 1] = jnp.sum(tapacc[t], axis=0, keepdims=True)
    ta = spread(n_row, "row", r, t_row, ta_s, ta_r)
    start(ta)

    for side in range(2):
        @pl.when(row_sends[side][1])
        def _():
            remote(
                row_send.at[side], row_recv.at[side], pr_s.at[side], pr_r.at[side],
                below if side == 0 else above,
            ).wait_recv()
            dst = lo if side == 0 else hi - edge
            @pl.loop(0, wide)
            def _(a):
                part[a, dst : dst + edge] += row_recv[side, a].astype(f32)

    def back_copy(side):
        return remote(
            col_send.at[side], col_recv.at[side], pc_s.at[side], pc_r.at[side],
            right if side == 0 else left,
        )

    for side in range(2):
        @pl.when(sends[side][0])
        def _():
            src = wide - reach if side == 0 else 0
            for a in range(reach):
                col_send[side, a] = part[src + a, lo:hi].astype(bf16)
            back_copy(side).start()

    wait(ta)
    t_dp[d] = jnp.sum(t_row[...], axis=0)
    tb = spread(n_dp, "dp", d, t_dp, tb_s, tb_r)
    start(tb)

    wait(gbc)
    mine = pl.multiple_of(mine + d * per_dp, 16)
    for s in range(0, per_dp, 64):
        acc = g32[pl.ds(pl.multiple_of(mine + s, 16), 64)]
        for i in range(n_dp - 1):
            acc = acc + g_rb[i, s : s + 64].astype(f32)
        g32[pl.ds(pl.multiple_of(mine + s, 16), 64)] = acc
        b2[s : s + 64] = acc.astype(bf16)
    gc = scatter(n_col, "col", c, per_col, b2, g_rc, gc_s, gc_r)
    start(gc)

    wait(tb)
    t_col[c] = jnp.sum(t_dp[...], axis=0)
    tc = spread(n_col, "col", c, t_col, tc_s, tc_r)
    start(tc)

    small_wait(1)
    slope_total = small_sums(1)
    dq = (
        lax.dot_general(
            slope_total, last, (((1,), (1,)), ((), ())), precision=highest,
            preferred_element_type=f32,
        )
        * s_four
    )
    dpooled = lax.dot_general(
        dq, pool32, (((1,), (1,)), ((), ())), precision=highest, preferred_element_type=f32
    )
    term[...] = dpooled * (1.0 / image_cells)
    own_mean = term[pl.ds(d, 1), :]
    scale = 1.0 / math.sqrt(image_cells * n_dp)
    pool_out[...] = scale * lax.dot_general(
        pooled, dq, (((0,), (0,)), ((), ())), precision=highest, preferred_element_type=f32
    )
    four_out[...] = scale * lax.dot_general(
        a_four, slope_total, (((0,), (0,)), ((), ())), precision=highest,
        preferred_element_type=f32,
    )

    wait(gc)
    mine = pl.multiple_of(mine + c * per_col, 16)
    acc = g32[pl.ds(mine, per_col)]
    for i in range(n_col - 1):
        acc = acc + g_rc[i].astype(f32)
    final[pl.ds(mine, per_col)] = acc.astype(bf16)
    hc = gather(n_col, "col", c, r * per_row + d * per_dp, per_col, hc_s, hc_r)
    start(hc)

    for side in range(2):
        @pl.when(sends[side][1])
        def _():
            back_copy(side).wait_recv()
            dst = reach if side == 0 else wide - 2 * reach
            for a in range(reach):
                part[dst + a, lo:hi] += col_recv[side, a].astype(f32)

    @pl.loop(0, blocks)
    def _(a):
        dx_out[a] = (part[a + reach, lo:hi] + dx0[a] + own_mean).astype(bf16)

    wait(hc)
    hb = gather(n_dp, "dp", d, r * per_row, per_dp, hb_s, hb_r)
    start(hb)
    wait(tc)
    taps_out[...] = scale * jnp.sum(t_col[...], axis=0)
    wait(hb)
    ha = gather(n_row, "row", r, 0, per_row, ha_s, ha_r)
    start(ha)

    for side in range(2):
        @pl.when(sends[side][0])
        def _():
            col_copy(side).wait_send()
            back_copy(side).wait_send()
        @pl.when(row_sends[side][0])
        def _():
            row_copy(side, 0).wait_send()
            for cside in range(2):
                @pl.when(sends[cside][1])
                def _():
                    row_copy(side, 1 + cside).wait_send()
            remote(
                row_send.at[side], row_recv.at[side], pr_s.at[side], pr_r.at[side],
                below if side == 0 else above,
            ).wait_send()

    wait(ha)

    @pl.loop(0, 8)
    def _(m):
        at = pl.ds(pl.multiple_of(m * ch, ch), ch)
        grads_out[at] = final[at].astype(f32) * scale


def x_flat(x_in):
    blocks, depth, ch = x_in.shape
    return x_in[...].reshape(blocks * depth, ch)


def shards(features, cotangent, w_one, w_point, taps, w_pool, w_proj):
    n_dp, n_row, n_col = (lax.axis_size(name) for name in ("dp", "row", "col"))
    total = n_dp * n_row * n_col
    batch, rows, cols, ch = features.shape
    blocks, depth = cols // unit, rows * unit
    wide, tall = blocks + 2 * reach, depth + 2 * edge
    count = rows * cols
    whole = 8 * ch
    per_row = whole // n_row
    per_dp = per_row // n_dp
    per_col = per_dp // n_col

    def split(x):
        x = x.reshape(rows, blocks, unit, ch)
        return jnp.transpose(x, (1, 0, 2, 3)).reshape(blocks, depth, ch)

    def join(x):
        x = x.reshape(blocks, rows, unit, ch)
        return jnp.transpose(x, (1, 0, 2, 3)).reshape(batch, rows, cols, ch)

    vmem = pl.BlockSpec(memory_space=pltpu.VMEM)
    dma = pltpu.SemaphoreType.DMA
    v = pltpu.VMEM
    scratch = [
        v((wide, tall, ch), bf16),
        v((wide, tall, ch), f32),
        v((wide, tall, ch), f32),
        v((4, count, ch), f32),
        v((4, count, ch), bf16),
        v((3, count, ch), bf16),
        v((count, ch), f32),
        v((count, ch), bf16),
        v((4, count, ch), bf16),
        v((3, count, ch), bf16),
        v((blocks, depth, ch), f32),
        v((2, total, 8, ch), f32),
        v((2, 8, ch), f32),
        v((8, ch), f32),
        v((27, 8, ch), f32),
        v((whole, ch), f32),
        v((whole, ch), bf16),
        v((n_row - 1, per_row, ch), bf16),
        v((per_row, ch), bf16),
        v((n_dp - 1, per_dp, ch), bf16),
        v((per_dp, ch), bf16),
        v((n_col - 1, per_col, ch), bf16),
        v((whole, ch), bf16),
        v((n_row, 32, ch), f32),
        v((n_dp, 32, ch), f32),
        v((n_col, 32, ch), f32),
        v((2, wide, edge, ch), bf16),
        v((2, wide, edge, ch), bf16),
        v((2, reach, depth, ch), bf16),
        v((2, reach, depth, ch), bf16),
    ]
    sems = [2, 2, 2, 2, 6, 6, 2, 2, 2, 2]
    sems += [n_row, n_row, n_dp, n_dp, n_col, n_col]
    sems += [n_row, n_row, n_dp, n_dp, n_col, n_col]
    sems += [n_row, n_row, n_dp, n_dp, n_col, n_col]
    scratch += [dma((n,)) for n in sems]
    image_cells = rows * cols * n_row * n_col
    shape = jax.ShapeDtypeStruct
    mixed, dx, grads, g_taps, g_pool, g_four = pl.pallas_call(
        functools.partial(kernel, n_dp, n_row, n_col, image_cells),
        out_shape=(
            shape((blocks, depth, ch), bf16),
            shape((blocks, depth, ch), bf16),
            shape((whole, ch), f32),
            shape((32, ch), f32),
            shape((ch, ch), f32),
            shape((ch, ch), f32),
        ),
        in_specs=[vmem] * 7,
        out_specs=[vmem] * 6,
        scratch_shapes=scratch,
        compiler_params=pltpu.CompilerParams(
            collective_id=0, has_side_effects=True, vmem_limit_bytes=58 << 20
        ),
        cost_estimate=pl.CostEstimate(
            flops=48 * count * ch * ch, bytes_accessed=8 << 20, transcendentals=10 * count * ch
        ),
    )(split(features), split(cotangent), w_one, w_point, taps, w_pool, w_proj)
    return (
        join(mixed),
        join(dx),
        grads[4 * ch : 5 * ch],
        grads[5 * ch :].reshape(3, ch, ch),
        g_taps[:27].reshape(3, 3, 3, ch),
        g_pool,
        jnp.concatenate([grads[: 4 * ch], g_four], axis=0),
    )


def solution(mesh):
    tiled = P("dp", "row", "col", None)
    return jax.shard_map(
        shards,
        mesh=mesh,
        in_specs=(tiled, tiled, P(), P(), P(), P(), P()),
        out_specs=(tiled, tiled, P(), P(), P(), P(), P()),
        check_vma=False,
    )
```

```python
import functools
import math

import jax
import jax.numpy as jnp
from jax import lax
from jax.experimental import pallas as pl
from jax.experimental.pallas import tpu as pltpu
from jax.sharding import PartitionSpec as P

unit = 6
margin = 18
reach = margin // unit
edge = 112
MESH = pl.DeviceIdType.MESH
f32 = jnp.float32
bf16 = jnp.bfloat16
highest = lax.Precision.HIGHEST


def silu_parts(value):
    sig = jax.nn.sigmoid(value)
    return value * sig, sig * (1.0 + value * (1.0 - sig))


def dot(a, b):
    return jnp.dot(a, b, preferred_element_type=f32)


def dot_nt(a, b):
    return lax.dot_general(a, b, (((1,), (1,)), ((), ())), preferred_element_type=f32)


def dot_tn(a, b):
    return lax.dot_general(a, b, (((0,), (0,)), ((), ())), preferred_element_type=f32)


def fold8(value):
    return jnp.sum(value.reshape(value.shape[0] // 8, 8, value.shape[1]), axis=0)


def kernel(
    n_dp, n_row, n_col, image_cells,
    x_in, cot, w_one, w_point, taps, w_pool, w_proj,
    mixed_out, dx_out, grads_out, taps_out, pool_out, four_out,
    line, flat, tile,
    xp, x32, part, slopes, acts, inner, pre_s, dpre_s, du_s, dz_s, dx0,
    slots, images, term, tapacc,
    g32, gb, g_ra, b1, g_rb, b2, g_rc, final,
    t_row, t_dp, t_col,
    row_send, row_recv, col_send, col_recv,
    sm_s, sm_r, xc_s, xc_r, xr_s, xr_r, pr_s, pr_r, pc_s, pc_r,
    ga_s, ga_r, gbs, gbr, gc_s, gc_r, ha_s, ha_r, hb_s, hb_r, hc_s, hc_r,
    ta_s, ta_r, tb_s, tb_r, tc_s, tc_r,
):
    d, r, c = lax.axis_index("dp"), lax.axis_index("row"), lax.axis_index("col")
    total = n_dp * n_row * n_col
    per = n_row * n_col
    me = (d * n_row + r) * n_col + c
    rows, cols, ch = x_in.shape
    blocks, depth = cols // unit, rows * unit
    wide = blocks + 2 * reach
    lo, hi = edge, edge + depth

    def peer(i):
        p = lax.rem(me + i, total)
        return {
            "dp": lax.div(p, per),
            "row": lax.rem(lax.div(p, n_col), n_row),
            "col": lax.rem(p, n_col),
        }

    def remote(src, dst, ss, rs, dev):
        return pltpu.make_async_remote_copy(
            src_ref=src, dst_ref=dst, send_sem=ss, recv_sem=rs, device_id=dev, device_id_type=MESH
        )

    barrier = pltpu.get_barrier_semaphore()

    xp[...] = jnp.zeros_like(xp)
    ones = jnp.zeros((8, ch), f32)
    split(x_in, line, tile)
    for a in range(blocks):
        block = tile[a]
        xp[reach + a, lo:hi] = block.astype(bf16)
        flat[a * depth : (a + 1) * depth] = block.astype(bf16)
        ones = ones + fold8(block)
    slots[0, me] = jnp.sum(ones, axis=0, keepdims=True)

    @pl.loop(1, total)
    def _(i):
        pl.semaphore_signal(barrier, inc=1, device_id=peer(i), device_id_type=MESH)

    pl.semaphore_wait(barrier, total - 1)

    right, left = {"col": lax.rem(c + 1, n_col)}, {"col": lax.rem(c + n_col - 1, n_col)}
    below, above = {"row": lax.rem(r + 1, n_row)}, {"row": lax.rem(r + n_row - 1, n_row)}
    has_right, has_left = c < n_col - 1, c > 0
    has_below, has_above = r < n_row - 1, r > 0

    def col_copy(side):
        src, dst = (wide - 2 * reach, 0) if side == 0 else (reach, wide - reach)
        mid = pl.ds(lo, depth)
        return remote(
            xp.at[pl.ds(src, reach), mid], xp.at[pl.ds(dst, reach), mid],
            xc_s.at[side], xc_r.at[side], right if side == 0 else left,
        )

    def row_copy(side, seg):
        span = (pl.ds(reach, blocks), pl.ds(0, reach), pl.ds(wide - reach, reach))[seg]
        src, dst = (hi - edge, 0) if side == 0 else (lo, hi)
        return remote(
            xp.at[span, pl.ds(src, edge)], xp.at[span, pl.ds(dst, edge)],
            xr_s.at[side * 3 + seg], xr_r.at[side * 3 + seg], below if side == 0 else above,
        )

    sends = ((has_right, has_left), (has_left, has_right))
    row_sends = ((has_below, has_above), (has_above, has_below))
    for side in range(2):
        @pl.when(sends[side][0])
        def _():
            col_copy(side).start()
    for side in range(2):
        @pl.when(row_sends[side][0])
        def _():
            row_copy(side, 0).start()

    def small_start(which):
        @pl.loop(1, total)
        def _(i):
            remote(
                slots.at[which, me], slots.at[which, me], sm_s.at[which], sm_r.at[which], peer(i)
            ).start()

    def small_wait(which):
        rest = slots.at[which, pl.ds(0, total - 1)]
        remote(rest, rest, sm_s.at[which], sm_r.at[which], peer(1)).wait()

    def small_sums(which):
        images[which] = jnp.zeros((8, ch), f32)
        for b in range(n_dp):
            images[which, b : b + 1] = jnp.sum(slots[which, b * per : (b + 1) * per], axis=0)
        return images[which]

    small_start(0)

    @pl.loop(0, blocks)
    def _(a):
        here = pl.ds(a * depth, depth)
        u = dot(flat[here], w_one[...])
        act, slope = silu_parts(u)
        act = act.astype(bf16)
        acts[0, here] = act
        slopes[0, here] = slope
        pre_s[here] = dot(act, w_proj[0:ch])

    @pl.loop(0, wide)
    def _(a):
        part[a] = jnp.zeros(part.shape[1:], f32)

    tapacc[...] = jnp.zeros_like(tapacc)
    split(cot, line, tile)

    for side in range(2):
        @pl.when(sends[side][1])
        def _():
            col_copy(side).wait_recv()
            for rside in range(2):
                @pl.when(row_sends[rside][0])
                def _():
                    row_copy(rside, 1 + side).start()

    for side in range(2):
        @pl.when(row_sends[side][1])
        def _():
            row_copy(side, 0).wait_recv()
            for cside in range(2):
                @pl.when(sends[cside][1])
                def _():
                    row_copy(side, 1 + cside).wait_recv()

    @pl.loop(0, wide)
    def _(a):
        x32[a] = xp[a].astype(f32)

    @pl.loop(0, blocks)
    def _(a):
        here = pl.ds(a * depth, depth)
        pre = pre_s[here]
        for k in range(3):
            acc = None
            for i in range(3):
                for j in range(3):
                    row = lo + 36 * (k + 1) * (i - 1)
                    win = x32[a + reach + (k + 1) * (j - 1), row : row + depth]
                    piece = win * taps[k, i, j : j + 1, :]
                    acc = piece if acc is None else acc + piece
            z = acc.astype(bf16)
            inner[k, here] = z
            act, slope = silu_parts(dot(z, w_point[k]))
            act = act.astype(bf16)
            acts[k + 1, here] = act
            slopes[k + 1, here] = slope
            pre = pre + dot(act, w_proj[(k + 1) * ch : (k + 2) * ch])
        pre_s[here] = pre

    small_wait(0)
    pooled = small_sums(0) * (1.0 / image_cells)
    pool32 = w_pool[...].astype(f32)
    last = w_proj[4 * ch : 5 * ch].astype(f32)
    q = jnp.dot(pooled, pool32, precision=highest, preferred_element_type=f32)
    a_four, s_four = silu_parts(q)
    term[...] = jnp.dot(a_four, last, precision=highest, preferred_element_type=f32)
    own_term = term[pl.ds(d, 1), :]

    folded = term
    folded[...] = jnp.zeros_like(folded)

    @pl.loop(0, blocks)
    def _(a):
        here = pl.ds(a * depth, depth)
        out, slope = silu_parts(pre_s[here] + own_term)
        dpre32 = tile[a] * slope
        tile[a] = out
        dpre = dpre32.astype(bf16)
        dpre_s[here] = dpre
        folded[...] += fold8(dpre.astype(f32))

    slots[1, me] = jnp.sum(folded[...], axis=0, keepdims=True)
    small_start(1)

    half = 4 * ch
    per_row, per_dp, per_col = (
        half // n_row,
        half // (n_row * n_dp),
        half // (n_row * n_dp * n_col),
    )
    bases = (0, r * per_row, r * per_row + d * per_dp, r * per_row + d * per_dp + c * per_col)
    levels = (
        ("row", n_row, r, per_row, gb, g_ra, ga_s, ga_r, ha_s, ha_r),
        ("dp", n_dp, d, per_dp, b1, g_rb, gbs, gbr, hb_s, hb_r),
        ("col", n_col, c, per_col, b2, g_rc, gc_s, gc_r, hc_s, hc_r),
    )

    def aligned(x):
        return pl.multiple_of(x, 16)

    def scatter(h, level):
        axis, n, at, size, src, dst, ss, rs, _, _ = levels[level]
        out = []
        for i in range(1, n):
            to = lax.rem(at + i, n)
            out.append(
                remote(
                    src.at[h, pl.ds(aligned(to * size), size)], dst.at[h, i - 1],
                    ss.at[h, i - 1], rs.at[h, i - 1], {axis: to},
                )
            )
        return out

    def add_up(h, level):
        axis, n, at, size, src, dst = levels[level][:6]
        step = min(size, 128)
        out = b1 if level == 0 else b2
        for p in range(0, size, step):
            there = pl.ds(aligned(bases[level + 1] + p), step)
            acc = g32[h, there]
            for i in range(n - 1):
                acc = acc + dst[h, i, p : p + step].astype(f32)
            if level == 2:
                final[h, there] = acc.astype(bf16)
            else:
                g32[h, there] = acc
                out[h, p : p + step] = acc.astype(bf16)

    def gather(h, level):
        axis, n, at, size, _, _, _, _, ss, rs = levels[level]
        own = final.at[h, pl.ds(aligned(bases[level + 1]), size)]
        return [
            remote(own, own, ss.at[h, i - 1], rs.at[h, i - 1], {axis: lax.rem(at + i, n)})
            for i in range(1, n)
        ]

    def spread(n, axis, at, buf, ss, rs):
        return [
            remote(buf.at[at], buf.at[at], ss.at[i - 1], rs.at[i - 1], {axis: lax.rem(at + i, n)})
            for i in range(1, n)
        ]

    def start(copies):
        for copy in copies:
            copy.start()

    def wait(copies):
        for copy in copies:
            copy.wait()

    for m in range(4):
        g = dot_tn(acts[m], dpre_s[...])
        g32[0, m * ch : (m + 1) * ch] = g
        gb[0, m * ch : (m + 1) * ch] = g.astype(bf16)
    start(scatter(0, 0))

    @pl.loop(0, blocks)
    def _(a):
        here = pl.ds(a * depth, depth)
        dpre = dpre_s[here]
        for m in range(4):
            dcat = dot_nt(dpre, w_proj[m * ch : (m + 1) * ch])
            du = (dcat * slopes[m, here]).astype(bf16)
            du_s[m, here] = du
            if m == 0:
                dx0[a] = dot_nt(du, w_one[...])
            else:
                dz_s[m - 1, here] = dot_nt(du, w_point[m - 1]).astype(bf16)

    wait(scatter(0, 0))
    add_up(0, 0)
    start(scatter(0, 1))
    for m in range(4):
        g = dot_tn(flat[...] if m == 0 else inner[m - 1], du_s[m])
        g32[1, m * ch : (m + 1) * ch] = g
        gb[1, m * ch : (m + 1) * ch] = g.astype(bf16)
    start(scatter(1, 0))

    def taps_back(a):
        here = pl.ds(a * depth, depth)
        for k in range(3):
            dz = dz_s[k, here].astype(f32)
            for i in range(3):
                for j in range(3):
                    row = lo + 36 * (k + 1) * (i - 1)
                    at = a + reach + (k + 1) * (j - 1)
                    tapacc[9 * k + 3 * i + j] += fold8(x32[at, row : row + depth] * dz)
                    part[at, row : row + depth] += dz * taps[k, i, j : j + 1, :]

    middle = blocks // 2

    @pl.loop(0, middle)
    def _(a):
        taps_back(a)

    wait(scatter(1, 0))
    add_up(1, 0)
    wait(scatter(0, 1))
    add_up(0, 1)
    start(scatter(0, 2))
    start(scatter(1, 1))

    @pl.loop(middle, blocks)
    def _(a):
        taps_back(a)

    def edge_copy(side):
        return remote(
            row_send.at[side], row_recv.at[side], pr_s.at[side], pr_r.at[side],
            below if side == 0 else above,
        )

    def back_copy(side):
        return remote(
            col_send.at[side], col_recv.at[side], pc_s.at[side], pc_r.at[side],
            right if side == 0 else left,
        )

    for side in range(2):
        @pl.when(row_sends[side][0])
        def _():
            src = hi if side == 0 else 0
            @pl.loop(0, wide)
            def _(a):
                row_send[side, a] = part[a, src : src + edge].astype(bf16)
            edge_copy(side).start()

    wait(scatter(0, 2))
    add_up(0, 2)
    start(gather(0, 2))

    t_row[r] = jnp.zeros(t_row.shape[1:], f32)
    for t in range(27):
        t_row[r, t : t + 1] = jnp.sum(tapacc[t], axis=0, keepdims=True)
    ta = spread(n_row, "row", r, t_row, ta_s, ta_r)
    start(ta)

    for side in range(2):
        @pl.when(row_sends[side][1])
        def _():
            edge_copy(side).wait_recv()
            dst = lo if side == 0 else hi - edge
            @pl.loop(0, wide)
            def _(a):
                part[a, dst : dst + edge] += row_recv[side, a].astype(f32)

    for side in range(2):
        @pl.when(sends[side][0])
        def _():
            src = wide - reach if side == 0 else 0
            for a in range(reach):
                col_send[side, a] = part[src + a, lo:hi].astype(bf16)
            back_copy(side).start()

    wait(scatter(1, 1))
    add_up(1, 1)
    start(scatter(1, 2))

    wait(ta)
    t_dp[d] = jnp.sum(t_row[...], axis=0)
    tb = spread(n_dp, "dp", d, t_dp, tb_s, tb_r)
    start(tb)

    join(tile, line, mixed_out)

    small_wait(1)
    slope_total = small_sums(1)
    dq = (
        lax.dot_general(
            slope_total, last, (((1,), (1,)), ((), ())), precision=highest,
            preferred_element_type=f32,
        )
        * s_four
    )
    dpooled = lax.dot_general(
        dq, pool32, (((1,), (1,)), ((), ())), precision=highest, preferred_element_type=f32
    )
    term[...] = dpooled * (1.0 / image_cells)
    own_mean = term[pl.ds(d, 1), :]
    scale = 1.0 / math.sqrt(image_cells * n_dp)
    pool_out[...] = scale * lax.dot_general(
        pooled, dq, (((0,), (0,)), ((), ())), precision=highest, preferred_element_type=f32
    )
    four_out[...] = scale * lax.dot_general(
        a_four, slope_total, (((0,), (0,)), ((), ())), precision=highest,
        preferred_element_type=f32,
    )

    wait(gather(0, 2))
    start(gather(0, 1))
    wait(tb)
    t_col[c] = jnp.sum(t_dp[...], axis=0)
    tc = spread(n_col, "col", c, t_col, tc_s, tc_r)
    start(tc)

    wait(scatter(1, 2))
    add_up(1, 2)
    start(gather(1, 2))
    wait(gather(0, 1))
    start(gather(0, 0))

    for side in range(2):
        @pl.when(sends[side][1])
        def _():
            back_copy(side).wait_recv()
            dst = reach if side == 0 else wide - 2 * reach
            for a in range(reach):
                part[dst + a, lo:hi] += col_recv[side, a].astype(f32)

    wait(gather(1, 2))
    start(gather(1, 1))

    @pl.loop(0, blocks)
    def _(a):
        tile[a] = part[a + reach, lo:hi] + dx0[a] + own_mean

    join(tile, line, dx_out)
    wait(tc)
    taps_out[...] = scale * jnp.sum(t_col[...], axis=0)
    wait(gather(0, 0))
    grads_out[0:half] = final[0]
    wait(gather(1, 1))
    start(gather(1, 0))

    for side in range(2):
        @pl.when(sends[side][0])
        def _():
            col_copy(side).wait_send()
            back_copy(side).wait_send()

        @pl.when(row_sends[side][0])
        def _():
            row_copy(side, 0).wait_send()
            for cside in range(2):
                @pl.when(sends[cside][1])
                def _():
                    row_copy(side, 1 + cside).wait_send()
            edge_copy(side).wait_send()

    wait(gather(1, 0))
    grads_out[half : 2 * half] = final[1]


def split(src, line, tile):
    rows, cols, _ = src.shape
    for p in range(rows):
        line[p % 2] = src[p].astype(f32)
        for a in range(cols // unit):
            tile[a, unit * p : unit * (p + 1)] = line[p % 2, unit * a : unit * (a + 1)]


def join(tile, line, dst):
    rows, cols, _ = dst.shape
    for p in range(rows):
        for a in range(cols // unit):
            line[p % 2, unit * a : unit * (a + 1)] = tile[a, unit * p : unit * (p + 1)]
        dst[p] = line[p % 2].astype(bf16)


def finish(
    scale, grads, g_taps, pool, four, mixed_in, dx_in,
    one, point, taps, pool_out, proj, mixed_out, dx_out, sems,
):
    ch = pool.shape[0]
    moves = (
        pltpu.make_async_copy(mixed_in, mixed_out, sems.at[0]),
        pltpu.make_async_copy(dx_in, dx_out, sems.at[1]),
        pltpu.make_async_copy(pool, pool_out, sems.at[2]),
    )
    for move in moves:
        move.start()
    proj[4 * ch : 5 * ch] = four[...]
    for m in range(8):
        block = grads[m * ch : (m + 1) * ch].astype(f32) * scale
        if m < 4:
            proj[m * ch : (m + 1) * ch] = block
        elif m == 4:
            one[...] = block
        else:
            point[m - 5] = block
    for t in range(27):
        taps[t // 9, t // 3 % 3, t % 3 : t % 3 + 1, :] = g_taps[t : t + 1, :]
    for move in moves:
        move.wait()


def shards(features, cotangent, w_one, w_point, taps, w_pool, w_proj):
    n_dp, n_row, n_col = (lax.axis_size(name) for name in ("dp", "row", "col"))
    total = n_dp * n_row * n_col
    batch, rows, cols, ch = features.shape
    blocks, depth = cols // unit, rows * unit
    wide, tall = blocks + 2 * reach, depth + 2 * edge
    count = rows * cols
    half = 4 * ch
    per_row = half // n_row
    per_dp = per_row // n_dp
    per_col = per_dp // n_col

    vmem = pl.BlockSpec(memory_space=pltpu.VMEM)
    dma = pltpu.SemaphoreType.DMA
    v = pltpu.VMEM
    scratch = [
        v((2, cols, ch), f32),
        v((count, ch), bf16),
        v((blocks, depth, ch), f32),
        v((wide, tall, ch), bf16),
        v((wide, tall, ch), f32),
        v((wide, tall, ch), f32),
        v((4, count, ch), f32),
        v((4, count, ch), bf16),
        v((3, count, ch), bf16),
        v((count, ch), f32),
        v((count, ch), bf16),
        v((4, count, ch), bf16),
        v((3, count, ch), bf16),
        v((blocks, depth, ch), f32),
        v((2, total, 1, ch), f32),
        v((2, 8, ch), f32),
        v((8, ch), f32),
        v((27, 8, ch), f32),
        v((2, half, ch), f32),
        v((2, half, ch), bf16),
        v((2, n_row - 1, per_row, ch), bf16),
        v((2, per_row, ch), bf16),
        v((2, n_dp - 1, per_dp, ch), bf16),
        v((2, per_dp, ch), bf16),
        v((2, n_col - 1, per_col, ch), bf16),
        v((2, half, ch), bf16),
        v((n_row, 32, ch), f32),
        v((n_dp, 32, ch), f32),
        v((n_col, 32, ch), f32),
        v((2, wide, edge, ch), bf16),
        v((2, wide, edge, ch), bf16),
        v((2, reach, depth, ch), bf16),
        v((2, reach, depth, ch), bf16),
    ]
    levels = [n_row, n_row, n_dp, n_dp, n_col, n_col]
    sems = [(n,) for n in (2, 2, 2, 2, 6, 6, 2, 2, 2, 2)]
    sems += [(2, n) for n in levels] * 2 + [(n,) for n in levels]
    scratch += [dma(n) for n in sems]
    image_cells = rows * cols * n_row * n_col
    shape = jax.ShapeDtypeStruct
    mixed, dx, grads, g_taps, g_pool, g_four = pl.pallas_call(
        functools.partial(kernel, n_dp, n_row, n_col, image_cells),
        out_shape=(
            shape((rows, cols, ch), bf16),
            shape((rows, cols, ch), bf16),
            shape((2 * half, ch), bf16),
            shape((32, ch), f32),
            shape((ch, ch), f32),
            shape((ch, ch), f32),
        ),
        in_specs=[vmem] * 7,
        out_specs=[vmem] * 6,
        scratch_shapes=scratch,
        compiler_params=pltpu.CompilerParams(
            collective_id=0, has_side_effects=True, vmem_limit_bytes=58 << 20
        ),
        cost_estimate=pl.CostEstimate(
            flops=48 * count * ch * ch, bytes_accessed=8 << 20, transcendentals=10 * count * ch
        ),
    )(
        features.reshape(rows, cols, ch), cotangent.reshape(rows, cols, ch),
        w_one, w_point, taps, w_pool, w_proj,
    )
    scale = 1.0 / math.sqrt(image_cells * n_dp)
    hbm = pl.BlockSpec(memory_space=pl.ANY)
    one, point, taps_out, pool, proj, mixed, dx = pl.pallas_call(
        functools.partial(finish, scale),
        out_shape=(
            shape((ch, ch), f32),
            shape((3, ch, ch), f32),
            shape((3, 3, 3, ch), f32),
            shape((ch, ch), f32),
            shape((5 * ch, ch), f32),
            shape((rows, cols, ch), bf16),
            shape((rows, cols, ch), bf16),
        ),
        in_specs=[vmem, vmem, hbm, vmem, hbm, hbm],
        out_specs=[vmem, vmem, vmem, hbm, vmem, hbm, hbm],
        scratch_shapes=[dma((3,))],
        compiler_params=pltpu.CompilerParams(vmem_limit_bytes=24 << 20),
        cost_estimate=pl.CostEstimate(flops=0, bytes_accessed=8 << 20, transcendentals=0),
    )(grads, g_taps, g_pool, g_four, mixed, dx)
    tiled = (batch, rows, cols, ch)
    return (mixed.reshape(tiled), dx.reshape(tiled), one, point, taps_out, pool, proj)


def solution(mesh):
    tiled = P("dp", "row", "col", None)
    return jax.shard_map(
        shards,
        mesh=mesh,
        in_specs=(tiled, tiled, P(), P(), P(), P(), P()),
        out_specs=(tiled, tiled, P(), P(), P(), P(), P()),
        check_vma=False,
    )
```

```python
import functools
import math

import jax
import jax.numpy as jnp
from jax import lax
from jax.experimental import pallas as pl
from jax.experimental.pallas import tpu as pltpu
from jax.sharding import PartitionSpec as P

unit = 6
margin = 18
reach = margin // unit
edge = 112
MESH = pl.DeviceIdType.MESH
f32 = jnp.float32
bf16 = jnp.bfloat16
highest = lax.Precision.HIGHEST


def silu_parts(value):
    sig = jax.nn.sigmoid(value)
    return value * sig, sig * (1.0 + value * (1.0 - sig))


def dot(a, b):
    return jnp.dot(a, b, preferred_element_type=f32)


def dot_nt(a, b):
    return lax.dot_general(a, b, (((1,), (1,)), ((), ())), preferred_element_type=f32)


def dot_tn(a, b):
    return lax.dot_general(a, b, (((0,), (0,)), ((), ())), preferred_element_type=f32)


def fold8(value):
    return jnp.sum(value.reshape(value.shape[0] // 8, 8, value.shape[1]), axis=0)


def kernel(
    n_dp, n_row, n_col, image_cells,
    x_in, cot, w_one, w_point, taps, w_pool, w_proj,
    mixed_out, dx_out, grads_out, taps_out, pool_out, four_out,
    line, flat, tile,
    xp, x32, part, slopes, acts, inner, pre_s, dpre_s, du_s, dz_s, dx0,
    s_row, s_col, s_dp, images, term, tapacc,
    g32, gb, g_ra, b1, g_rb, b2, g_rc, final,
    t_row, t_dp, t_col,
    row_send, row_recv, col_send, col_recv,
    xc_s, xc_r, xr_s, xr_r, pr_s, pr_r, pc_s, pc_r,
    ga_s, ga_r, gbs, gbr, gc_s, gc_r, ha_s, ha_r, hb_s, hb_r, hc_s, hc_r,
    ta_s, ta_r, tb_s, tb_r, tc_s, tc_r,
    sa_s, sa_r, sb_s, sb_r, sc_s, sc_r,
):
    d, r, c = lax.axis_index("dp"), lax.axis_index("row"), lax.axis_index("col")
    rows, cols, ch = x_in.shape
    blocks, depth = cols // unit, rows * unit
    wide = blocks + 2 * reach
    lo, hi = edge, edge + depth

    def remote(src, dst, ss, rs, dev):
        return pltpu.make_async_remote_copy(
            src_ref=src, dst_ref=dst, send_sem=ss, recv_sem=rs, device_id=dev, device_id_type=MESH
        )

    barrier = pltpu.get_barrier_semaphore()

    xp[...] = jnp.zeros_like(xp)
    ones = jnp.zeros((8, ch), f32)
    split(x_in, line, tile)
    for a in range(blocks):
        block = tile[a]
        xp[reach + a, lo:hi] = block.astype(bf16)
        flat[a * depth : (a + 1) * depth] = block.astype(bf16)
        ones = ones + fold8(block)
    s_row[0, r] = jnp.sum(ones, axis=0, keepdims=True)

    for axis, n, at in (("col", n_col, c), ("row", n_row, r), ("dp", n_dp, d)):
        for i in range(1, n):
            pl.semaphore_signal(
                barrier, inc=1, device_id={axis: lax.rem(at + i, n)}, device_id_type=MESH
            )

    pl.semaphore_wait(barrier, n_col + n_row + n_dp - 3)

    right, left = {"col": lax.rem(c + 1, n_col)}, {"col": lax.rem(c + n_col - 1, n_col)}
    below, above = {"row": lax.rem(r + 1, n_row)}, {"row": lax.rem(r + n_row - 1, n_row)}
    has_right, has_left = c < n_col - 1, c > 0
    has_below, has_above = r < n_row - 1, r > 0

    def col_copy(side):
        src, dst = (wide - 2 * reach, 0) if side == 0 else (reach, wide - reach)
        mid = pl.ds(lo, depth)
        return remote(
            xp.at[pl.ds(src, reach), mid], xp.at[pl.ds(dst, reach), mid],
            xc_s.at[side], xc_r.at[side], right if side == 0 else left,
        )

    def row_copy(side, seg):
        span = (pl.ds(reach, blocks), pl.ds(0, reach), pl.ds(wide - reach, reach))[seg]
        src, dst = (hi - edge, 0) if side == 0 else (lo, hi)
        return remote(
            xp.at[span, pl.ds(src, edge)], xp.at[span, pl.ds(dst, edge)],
            xr_s.at[side * 3 + seg], xr_r.at[side * 3 + seg], below if side == 0 else above,
        )

    sends = ((has_right, has_left), (has_left, has_right))
    row_sends = ((has_below, has_above), (has_above, has_below))
    for side in range(2):
        @pl.when(sends[side][0])
        def _():
            col_copy(side).start()
    for side in range(2):
        @pl.when(row_sends[side][0])
        def _():
            row_copy(side, 0).start()

    def spread(n, axis, at, buf, ss, rs, pre=()):
        own = buf.at[(*pre, at)]
        return [
            remote(own, own, ss.at[(*pre, i - 1)], rs.at[(*pre, i - 1)], {axis: lax.rem(at + i, n)})
            for i in range(1, n)
        ]

    def start(copies):
        for copy in copies:
            copy.start()

    def wait(copies):
        for copy in copies:
            copy.wait()

    def small(level, which):
        if level == 0:
            return spread(n_row, "row", r, s_row, sa_s, sa_r, (which,))
        if level == 1:
            return spread(n_col, "col", c, s_col, sc_s, sc_r, (which,))
        return spread(n_dp, "dp", d, s_dp, sb_s, sb_r, (which,))

    def small_next(level, which):
        wait(small(level, which))
        if level == 0:
            s_col[which, c] = jnp.sum(s_row[which], axis=0)
        else:
            s_dp[which, d] = jnp.sum(s_col[which], axis=0)
        start(small(level + 1, which))

    def small_sums(which):
        wait(small(2, which))
        images[which] = jnp.zeros((8, ch), f32)
        for b in range(n_dp):
            images[which, b : b + 1] = s_dp[which, b]
        return images[which]

    start(small(0, 0))

    @pl.loop(0, blocks)
    def _(a):
        here = pl.ds(a * depth, depth)
        u = dot(flat[here], w_one[...])
        act, slope = silu_parts(u)
        act = act.astype(bf16)
        acts[0, here] = act
        slopes[0, here] = slope
        pre_s[here] = dot(act, w_proj[0:ch])

    small_next(0, 0)

    @pl.loop(0, wide)
    def _(a):
        part[a] = jnp.zeros(part.shape[1:], f32)

    tapacc[...] = jnp.zeros_like(tapacc)
    split(cot, line, tile)
    small_next(1, 0)

    for side in range(2):
        @pl.when(sends[side][1])
        def _():
            col_copy(side).wait_recv()
            for rside in range(2):
                @pl.when(row_sends[rside][0])
                def _():
                    row_copy(rside, 1 + side).start()

    for side in range(2):
        @pl.when(row_sends[side][1])
        def _():
            row_copy(side, 0).wait_recv()
            for cside in range(2):
                @pl.when(sends[cside][1])
                def _():
                    row_copy(side, 1 + cside).wait_recv()

    @pl.loop(0, wide)
    def _(a):
        x32[a] = xp[a].astype(f32)

    @pl.loop(0, blocks)
    def _(a):
        here = pl.ds(a * depth, depth)
        pre = pre_s[here]
        for k in range(3):
            acc = None
            for i in range(3):
                for j in range(3):
                    row = lo + 36 * (k + 1) * (i - 1)
                    win = x32[a + reach + (k + 1) * (j - 1), row : row + depth]
                    piece = win * taps[k, i, j : j + 1, :]
                    acc = piece if acc is None else acc + piece
            z = acc.astype(bf16)
            inner[k, here] = z
            act, slope = silu_parts(dot(z, w_point[k]))
            act = act.astype(bf16)
            acts[k + 1, here] = act
            slopes[k + 1, here] = slope
            pre = pre + dot(act, w_proj[(k + 1) * ch : (k + 2) * ch])
        pre_s[here] = pre

    pooled = small_sums(0) * (1.0 / image_cells)
    pool32 = w_pool[...].astype(f32)
    last = w_proj[4 * ch : 5 * ch].astype(f32)
    q = jnp.dot(pooled, pool32, precision=highest, preferred_element_type=f32)
    a_four, s_four = silu_parts(q)
    term[...] = jnp.dot(a_four, last, precision=highest, preferred_element_type=f32)
    own_term = term[pl.ds(d, 1), :]

    folded = term
    folded[...] = jnp.zeros_like(folded)

    @pl.loop(0, blocks)
    def _(a):
        here = pl.ds(a * depth, depth)
        out, slope = silu_parts(pre_s[here] + own_term)
        dpre32 = tile[a] * slope
        tile[a] = out
        dpre = dpre32.astype(bf16)
        dpre_s[here] = dpre
        folded[...] += fold8(dpre.astype(f32))

    s_row[1, r] = jnp.sum(folded[...], axis=0, keepdims=True)
    start(small(0, 1))

    half = 4 * ch
    per_row, per_dp, per_col = (
        half // n_row,
        half // (n_row * n_dp),
        half // (n_row * n_dp * n_col),
    )
    bases = (0, r * per_row, r * per_row + d * per_dp, r * per_row + d * per_dp + c * per_col)
    levels = (
        ("row", n_row, r, per_row, gb, g_ra, ga_s, ga_r, ha_s, ha_r),
        ("dp", n_dp, d, per_dp, b1, g_rb, gbs, gbr, hb_s, hb_r),
        ("col", n_col, c, per_col, b2, g_rc, gc_s, gc_r, hc_s, hc_r),
    )

    def aligned(x):
        return pl.multiple_of(x, 16)

    def scatter(h, level):
        axis, n, at, size, src, dst, ss, rs, _, _ = levels[level]
        out = []
        for i in range(1, n):
            to = lax.rem(at + i, n)
            out.append(
                remote(
                    src.at[h, pl.ds(aligned(to * size), size)], dst.at[h, i - 1],
                    ss.at[h, i - 1], rs.at[h, i - 1], {axis: to},
                )
            )
        return out

    def add_up(h, level):
        axis, n, at, size, src, dst = levels[level][:6]
        step = min(size, 128)
        out = b1 if level == 0 else b2
        for p in range(0, size, step):
            there = pl.ds(aligned(bases[level + 1] + p), step)
            acc = g32[h, there]
            for i in range(n - 1):
                acc = acc + dst[h, i, p : p + step].astype(f32)
            if level == 2:
                final[h, there] = acc.astype(bf16)
            else:
                g32[h, there] = acc
                out[h, p : p + step] = acc.astype(bf16)

    def gather(h, level):
        axis, n, at, size, _, _, _, _, ss, rs = levels[level]
        own = final.at[h, pl.ds(aligned(bases[level + 1]), size)]
        return [
            remote(own, own, ss.at[h, i - 1], rs.at[h, i - 1], {axis: lax.rem(at + i, n)})
            for i in range(1, n)
        ]

    for m in range(4):
        g = dot_tn(acts[m], dpre_s[...])
        g32[0, m * ch : (m + 1) * ch] = g
        gb[0, m * ch : (m + 1) * ch] = g.astype(bf16)
    start(scatter(0, 0))

    @pl.loop(0, blocks)
    def _(a):
        here = pl.ds(a * depth, depth)
        dpre = dpre_s[here]
        for m in range(4):
            dcat = dot_nt(dpre, w_proj[m * ch : (m + 1) * ch])
            du = (dcat * slopes[m, here]).astype(bf16)
            du_s[m, here] = du
            if m == 0:
                dx0[a] = dot_nt(du, w_one[...])
            else:
                dz_s[m - 1, here] = dot_nt(du, w_point[m - 1]).astype(bf16)

    small_next(0, 1)
    wait(scatter(0, 0))
    add_up(0, 0)
    start(scatter(0, 1))
    for m in range(4):
        g = dot_tn(flat[...] if m == 0 else inner[m - 1], du_s[m])
        g32[1, m * ch : (m + 1) * ch] = g
        gb[1, m * ch : (m + 1) * ch] = g.astype(bf16)
    start(scatter(1, 0))

    def taps_back(a):
        here = pl.ds(a * depth, depth)
        for k in range(3):
            dz = dz_s[k, here].astype(f32)
            for i in range(3):
                for j in range(3):
                    row = lo + 36 * (k + 1) * (i - 1)
                    at = a + reach + (k + 1) * (j - 1)
                    tapacc[9 * k + 3 * i + j] += fold8(x32[at, row : row + depth] * dz)
                    part[at, row : row + depth] += dz * taps[k, i, j : j + 1, :]

    middle = blocks // 2

    @pl.loop(0, middle)
    def _(a):
        taps_back(a)

    small_next(1, 1)
    wait(scatter(1, 0))
    add_up(1, 0)
    wait(scatter(0, 1))
    add_up(0, 1)
    start(scatter(0, 2))
    start(scatter(1, 1))

    @pl.loop(middle, blocks)
    def _(a):
        taps_back(a)

    def edge_copy(side):
        return remote(
            row_send.at[side], row_recv.at[side], pr_s.at[side], pr_r.at[side],
            below if side == 0 else above,
        )

    def back_copy(side):
        return remote(
            col_send.at[side], col_recv.at[side], pc_s.at[side], pc_r.at[side],
            right if side == 0 else left,
        )

    for side in range(2):
        @pl.when(row_sends[side][0])
        def _():
            src = hi if side == 0 else 0
            @pl.loop(0, wide)
            def _(a):
                row_send[side, a] = part[a, src : src + edge].astype(bf16)
            edge_copy(side).start()

    wait(scatter(0, 2))
    add_up(0, 2)
    start(gather(0, 2))

    t_row[r] = jnp.zeros(t_row.shape[1:], f32)
    for t in range(27):
        t_row[r, t : t + 1] = jnp.sum(tapacc[t], axis=0, keepdims=True)
    ta = spread(n_row, "row", r, t_row, ta_s, ta_r)
    start(ta)

    for side in range(2):
        @pl.when(row_sends[side][1])
        def _():
            edge_copy(side).wait_recv()
            dst = lo if side == 0 else hi - edge
            @pl.loop(0, wide)
            def _(a):
                part[a, dst : dst + edge] += row_recv[side, a].astype(f32)

    for side in range(2):
        @pl.when(sends[side][0])
        def _():
            src = wide - reach if side == 0 else 0
            for a in range(reach):
                col_send[side, a] = part[src + a, lo:hi].astype(bf16)
            back_copy(side).start()

    wait(scatter(1, 1))
    add_up(1, 1)
    start(scatter(1, 2))

    wait(ta)
    t_dp[d] = jnp.sum(t_row[...], axis=0)
    tb = spread(n_dp, "dp", d, t_dp, tb_s, tb_r)
    start(tb)

    join(tile, line, mixed_out)

    slope_total = small_sums(1)
    dq = (
        lax.dot_general(
            slope_total, last, (((1,), (1,)), ((), ())), precision=highest,
            preferred_element_type=f32,
        )
        * s_four
    )
    dpooled = lax.dot_general(
        dq, pool32, (((1,), (1,)), ((), ())), precision=highest, preferred_element_type=f32
    )
    term[...] = dpooled * (1.0 / image_cells)
    own_mean = term[pl.ds(d, 1), :]
    scale = 1.0 / math.sqrt(image_cells * n_dp)
    pool_out[...] = scale * lax.dot_general(
        pooled, dq, (((0,), (0,)), ((), ())), precision=highest, preferred_element_type=f32
    )
    four_out[...] = scale * lax.dot_general(
        a_four, slope_total, (((0,), (0,)), ((), ())), precision=highest,
        preferred_element_type=f32,
    )

    wait(gather(0, 2))
    start(gather(0, 1))
    wait(tb)
    t_col[c] = jnp.sum(t_dp[...], axis=0)
    tc = spread(n_col, "col", c, t_col, tc_s, tc_r)
    start(tc)

    wait(scatter(1, 2))
    add_up(1, 2)
    start(gather(1, 2))
    wait(gather(0, 1))
    start(gather(0, 0))

    for side in range(2):
        @pl.when(sends[side][1])
        def _():
            back_copy(side).wait_recv()
            dst = reach if side == 0 else wide - 2 * reach
            for a in range(reach):
                part[dst + a, lo:hi] += col_recv[side, a].astype(f32)

    wait(gather(1, 2))
    start(gather(1, 1))

    @pl.loop(0, blocks)
    def _(a):
        tile[a] = part[a + reach, lo:hi] + dx0[a] + own_mean

    join(tile, line, dx_out)
    wait(tc)
    taps_out[...] = scale * jnp.sum(t_col[...], axis=0)
    wait(gather(0, 0))
    grads_out[0:half] = final[0]
    wait(gather(1, 1))
    start(gather(1, 0))

    for side in range(2):
        @pl.when(sends[side][0])
        def _():
            col_copy(side).wait_send()
            back_copy(side).wait_send()

        @pl.when(row_sends[side][0])
        def _():
            row_copy(side, 0).wait_send()
            for cside in range(2):
                @pl.when(sends[cside][1])
                def _():
                    row_copy(side, 1 + cside).wait_send()
            edge_copy(side).wait_send()

    wait(gather(1, 0))
    grads_out[half : 2 * half] = final[1]


def split(src, line, tile):
    rows, cols, _ = src.shape
    for p in range(rows):
        line[p % 2] = src[p].astype(f32)
        for a in range(cols // unit):
            tile[a, unit * p : unit * (p + 1)] = line[p % 2, unit * a : unit * (a + 1)]


def join(tile, line, dst):
    rows, cols, _ = dst.shape
    for p in range(rows):
        for a in range(cols // unit):
            line[p % 2, unit * a : unit * (a + 1)] = tile[a, unit * p : unit * (p + 1)]
        dst[p] = line[p % 2].astype(bf16)


def finish(
    scale, grads, g_taps, pool, four, mixed_in, dx_in,
    one, point, taps, pool_out, proj, mixed_out, dx_out, sems,
):
    ch = pool.shape[0]
    moves = (
        pltpu.make_async_copy(mixed_in, mixed_out, sems.at[0]),
        pltpu.make_async_copy(dx_in, dx_out, sems.at[1]),
        pltpu.make_async_copy(pool, pool_out, sems.at[2]),
    )
    for move in moves:
        move.start()
    proj[4 * ch : 5 * ch] = four[...]
    for m in range(8):
        block = grads[m * ch : (m + 1) * ch].astype(f32) * scale
        if m < 4:
            proj[m * ch : (m + 1) * ch] = block
        elif m == 4:
            one[...] = block
        else:
            point[m - 5] = block
    for t in range(27):
        taps[t // 9, t // 3 % 3, t % 3 : t % 3 + 1, :] = g_taps[t : t + 1, :]
    for move in moves:
        move.wait()


def shards(features, cotangent, w_one, w_point, taps, w_pool, w_proj):
    n_dp, n_row, n_col = (lax.axis_size(name) for name in ("dp", "row", "col"))
    batch, rows, cols, ch = features.shape
    blocks, depth = cols // unit, rows * unit
    wide, tall = blocks + 2 * reach, depth + 2 * edge
    count = rows * cols
    half = 4 * ch
    per_row = half // n_row
    per_dp = per_row // n_dp
    per_col = per_dp // n_col

    vmem = pl.BlockSpec(memory_space=pltpu.VMEM)
    dma = pltpu.SemaphoreType.DMA
    v = pltpu.VMEM
    scratch = [
        v((2, cols, ch), f32),
        v((count, ch), bf16),
        v((blocks, depth, ch), f32),
        v((wide, tall, ch), bf16),
        v((wide, tall, ch), f32),
        v((wide, tall, ch), f32),
        v((4, count, ch), f32),
        v((4, count, ch), bf16),
        v((3, count, ch), bf16),
        v((count, ch), f32),
        v((count, ch), bf16),
        v((4, count, ch), bf16),
        v((3, count, ch), bf16),
        v((blocks, depth, ch), f32),
        v((2, n_row, 1, ch), f32),
        v((2, n_col, 1, ch), f32),
        v((2, n_dp, 1, ch), f32),
        v((2, 8, ch), f32),
        v((8, ch), f32),
        v((27, 8, ch), f32),
        v((2, half, ch), f32),
        v((2, half, ch), bf16),
        v((2, n_row - 1, per_row, ch), bf16),
        v((2, per_row, ch), bf16),
        v((2, n_dp - 1, per_dp, ch), bf16),
        v((2, per_dp, ch), bf16),
        v((2, n_col - 1, per_col, ch), bf16),
        v((2, half, ch), bf16),
        v((n_row, 32, ch), f32),
        v((n_dp, 32, ch), f32),
        v((n_col, 32, ch), f32),
        v((2, wide, edge, ch), bf16),
        v((2, wide, edge, ch), bf16),
        v((2, reach, depth, ch), bf16),
        v((2, reach, depth, ch), bf16),
    ]
    levels = [n_row, n_row, n_dp, n_dp, n_col, n_col]
    sems = [(n,) for n in (2, 2, 6, 6, 2, 2, 2, 2)]
    sems += [(2, n) for n in levels] * 2 + [(n,) for n in levels] + [(2, n) for n in levels]
    scratch += [dma(n) for n in sems]
    image_cells = rows * cols * n_row * n_col
    shape = jax.ShapeDtypeStruct
    mixed, dx, grads, g_taps, g_pool, g_four = pl.pallas_call(
        functools.partial(kernel, n_dp, n_row, n_col, image_cells),
        out_shape=(
            shape((rows, cols, ch), bf16),
            shape((rows, cols, ch), bf16),
            shape((2 * half, ch), bf16),
            shape((32, ch), f32),
            shape((ch, ch), f32),
            shape((ch, ch), f32),
        ),
        in_specs=[vmem] * 7,
        out_specs=[vmem] * 6,
        scratch_shapes=scratch,
        compiler_params=pltpu.CompilerParams(
            collective_id=0, has_side_effects=True, vmem_limit_bytes=58 << 20
        ),
        cost_estimate=pl.CostEstimate(
            flops=48 * count * ch * ch, bytes_accessed=8 << 20, transcendentals=10 * count * ch
        ),
    )(
        features.reshape(rows, cols, ch), cotangent.reshape(rows, cols, ch),
        w_one, w_point, taps, w_pool, w_proj,
    )
    scale = 1.0 / math.sqrt(image_cells * n_dp)
    hbm = pl.BlockSpec(memory_space=pl.ANY)
    one, point, taps_out, pool, proj, mixed, dx = pl.pallas_call(
        functools.partial(finish, scale),
        out_shape=(
            shape((ch, ch), f32),
            shape((3, ch, ch), f32),
            shape((3, 3, 3, ch), f32),
            shape((ch, ch), f32),
            shape((5 * ch, ch), f32),
            shape((rows, cols, ch), bf16),
            shape((rows, cols, ch), bf16),
        ),
        in_specs=[vmem, vmem, hbm, vmem, hbm, hbm],
        out_specs=[vmem, vmem, vmem, hbm, vmem, hbm, hbm],
        scratch_shapes=[dma((3,))],
        compiler_params=pltpu.CompilerParams(vmem_limit_bytes=58 << 20),
        cost_estimate=pl.CostEstimate(flops=0, bytes_accessed=8 << 20, transcendentals=0),
    )(grads, g_taps, g_pool, g_four, mixed, dx)
    tiled = (batch, rows, cols, ch)
    return (mixed.reshape(tiled), dx.reshape(tiled), one, point, taps_out, pool, proj)


def solution(mesh):
    tiled = P("dp", "row", "col", None)
    return jax.shard_map(
        shards,
        mesh=mesh,
        in_specs=(tiled, tiled, P(), P(), P(), P(), P()),
        out_specs=(tiled, tiled, P(), P(), P(), P(), P()),
        check_vma=False,
    )
```
